32 devices in a mesh: cuts: 2 (over x), tile: 16 (over z, y, core).
Axes of the slice: x: 2, y: 2, z: 4, core: 2. Of those that a mesh axis runs over, the one named last changes fastest.
Arguments:
- trans_real: float32 [2, 4096, 256], P('cuts', 'tile'), may hold values from 0.6 to 1.4
- trans_imag: float32 [2, 4096, 256], P('cuts', 'tile'), may hold values from -1.5 to 1.5
- probe_real: bfloat16 [128, 128], replicated, may hold values from -6 to 6
- probe_imag: bfloat16 [128, 128], replicated, may hold values from -6 to 6
- offsets: int32 [2, 512], P(None, 'tile'), may hold values from 0 to 128
- pattern_index: int32 [512], P('tile'), may hold values from 0 to 511, as said below
- measured: bfloat16 [512, 128, 128], P('tile'), may hold values from 0.19921875 to 3
Outputs:
- object_grad: float32 [2, 2, 4096, 256], P(None, 'cuts', 'tile')
The draws below stay inside these ranges and needn't reach their ends.
Inputs may be any that keep to these rules, and one draw needn't show every extreme that they name: `pattern_index`: each row of measured is named by exactly one position; row r is stored with tile r // 32. Of the positions of one tile at most 2 have patterns stored with any one tile, and every tile has exactly 2 with some tile.
All inputs are finite; a program needn't handle non-finite values.
Results may differ from the reference program's by a relative error of at most 0.015.
The reference program's roundings to bfloat16 on the way count: a program that leaves them out, or rounds other values in their place, can miss the bound.
Values may be sent and summed in bfloat16 or wider, within the bound.
A program may use at most 64 MiB of HBM per device.

```python
import math
import jax
import jax.numpy as jnp
from jax import lax

WIN = 128
PATCH = 256
POS_TILE = 32
SLICES = 2
POSITIONS = 512
N_TILE = 16


def draw_pattern_index(key, part):
    tile_count = N_TILE
    per_tile = POS_TILE
    unit_size = (per_tile + tile_count - 1) // tile_count
    groups = per_tile // unit_size
    key_shift = jax.random.fold_in(key, 23)
    key_order = jax.random.fold_in(key, 37)
    candidates = jnp.arange(tile_count, dtype=jnp.int32)
    ranking = jax.random.permutation(key_shift, tile_count).astype(jnp.int32)
    forced = (candidates == tile_count // 2) | (candidates == 1 % tile_count) | (candidates == tile_count - 1)
    priority = ranking - 3 * tile_count * forced.astype(jnp.int32)
    shifts = jnp.argsort(priority, stable=True)[:groups].astype(jnp.int32)
    ordinal = jnp.arange(per_tile, dtype=jnp.int32)
    member = ordinal // unit_size
    shift_of = jnp.take(shifts, member)
    devices = jnp.arange(tile_count, dtype=jnp.int32)
    owners = (devices[:, None] + shift_of[None, :]) % tile_count
    rows_index = owners * per_tile + ordinal[None, :]
    scores = jax.random.randint(key_order, (tile_count, per_tile), 0, 1 << 20) * per_tile + ordinal[None, :]
    order_rows = jnp.argsort(scores, axis=1, stable=True)
    shuffled = jnp.take_along_axis(rows_index, order_rows, axis=1)
    return shuffled.reshape(-1).astype(jnp.int32)


def set_ends(drawn, own_key, low, high):
    shape = drawn.shape
    place = [jax.random.randint(jax.random.fold_in(own_key, axis), (), 0, shape[axis]) for axis in range(len(shape))]
    drawn = drawn.at[tuple(place)].set(low)
    longest = shape.index(max(shape))
    place[longest] = (place[longest] + 1) % shape[longest]
    return drawn.at[tuple(place)].set(high)


def steps_of(key, shape, pieces, low, top_value):
    def one(axis_at, blocks):
        heights = jax.random.uniform(jax.random.fold_in(jax.random.fold_in(key, 6), axis_at), (blocks,), jnp.float32, low / len(pieces), top_value / len(pieces))
        return jnp.repeat(jnp.exp(heights), shape[axis_at] // blocks).reshape((-1,) + (1,) * (len(shape) - axis_at - 1))

    level = one(*pieces[0])
    for cut in pieces[1:]:
        level = level * one(*cut)
    return level


def centred(key, shape, width, reach, cuts=(), kind=jnp.bfloat16):
    values = jax.random.normal(key, shape, jnp.float32) * width
    if len(cuts) > 0:
        values = steps_of(key, shape, cuts, -0.22, 0.18) * values
    return jnp.clip(values, min=-reach, max=reach).astype(kind)


def setup_inputs(seed: int = 0) -> dict:
    key_list = jax.random.split(jax.random.key(seed), 8)
    trans_real = jnp.clip(1.0 + 0.08 * jax.random.normal(key_list[0], (SLICES, N_TILE * PATCH, PATCH), jnp.float32), 0.6, 1.4)
    trans_imag = centred(key_list[1], (SLICES, N_TILE * PATCH, PATCH), 0.3, 1.5, ((0, 2), (1, 16)), jnp.float32)
    probe_real = centred(key_list[2], (WIN, WIN), 1.0, 6.0)
    probe_imag = centred(key_list[3], (WIN, WIN), 1.0, 6.0)
    offsets = set_ends(jax.random.randint(key_list[4], (2, POSITIONS), 0, PATCH - WIN + 1), jax.random.fold_in(key_list[4], 1), 0, PATCH - WIN).astype(jnp.int32)
    pattern_index = draw_pattern_index(jax.random.fold_in(key_list[7], 71), 0)
    measured = jnp.clip(jnp.exp(math.log(3.0) - 2.7119641 * jax.random.uniform(key_list[6], (POSITIONS, WIN, WIN), jnp.float32) ** steps_of(key_list[6], (POSITIONS, WIN, WIN), ((0, 16),), -0.2, 0.2)), 0.19921875, 3.0).astype(jnp.bfloat16)
    return {"trans_real": trans_real, "trans_imag": trans_imag, "probe_real": probe_real, "probe_imag": probe_imag, "offsets": offsets, "pattern_index": pattern_index, "measured": measured}


fresnel_strength = 9.0
softening = 0.01

def tables(extent):
    indices = jnp.arange(extent, dtype=jnp.int32)
    products = indices[:, None] * indices[None, :] % extent
    angles = products.astype(jnp.float32) * (2.0 * math.pi / extent)
    cosine = jnp.cos(angles)
    sines = jnp.sin(angles)
    frequency = jnp.where(indices < (extent + 1) // 2, indices, indices - extent).astype(jnp.float32) / extent
    phases = -fresnel_strength * frequency * frequency
    kernel_real = jnp.cos(phases)
    kernel_imag = jnp.sin(phases)
    scaled_real = cosine * kernel_real[None, :] - sines * kernel_imag[None, :]
    scaled_imag = cosine * kernel_imag[None, :] + sines * kernel_real[None, :]
    highest = lax.Precision.HIGHEST
    prop_real = (jnp.dot(scaled_real, cosine, precision=highest) + jnp.dot(scaled_imag, sines, precision=highest)) / extent
    prop_imag = (jnp.dot(scaled_imag, cosine, precision=highest) - jnp.dot(scaled_real, sines, precision=highest)) / extent
    norming = 1.0 / math.sqrt(extent)
    return (prop_real.astype(jnp.bfloat16), prop_imag.astype(jnp.bfloat16), (cosine * norming).astype(jnp.bfloat16), (-sines * norming).astype(jnp.bfloat16))

def left_product(matrix, field):
    return jnp.einsum('ab,nbc->nac', matrix.astype(jnp.float32), field.astype(jnp.float32))

def right_product(field, matrix):
    return jnp.einsum('nab,bc->nac', field.astype(jnp.float32), matrix.astype(jnp.float32))

def apply_both(mat_real, mat_imag, field_real, field_imag):
    mid_real = (left_product(mat_real, field_real) - left_product(mat_imag, field_imag)).astype(jnp.bfloat16)
    mid_imag = (left_product(mat_real, field_imag) + left_product(mat_imag, field_real)).astype(jnp.bfloat16)
    end_real = right_product(mid_real, mat_real) - right_product(mid_imag, mat_imag)
    end_imag = right_product(mid_real, mat_imag) + right_product(mid_imag, mat_real)
    return (end_real, end_imag)

def windows(patch_grid, offset_sel, extent):

    def cut_one(row_at, col_at):
        return lax.dynamic_slice(patch_grid, (row_at, col_at), (extent, extent))
    return jax.vmap(cut_one)(offset_sel[0], offset_sel[1])

def accumulate(patch_grid, contrib, offset_sel, extent):

    def add_one(item, acc):
        row_at = offset_sel[0, item]
        col_at = offset_sel[1, item]
        current = lax.dynamic_slice(acc, (row_at, col_at), (extent, extent))
        return lax.dynamic_update_slice(acc, current + contrib[item], (row_at, col_at))
    return lax.fori_loop(0, contrib.shape[0], add_one, patch_grid)

def forward_slice(win_real, win_imag, wave_real, wave_imag, prop_real, prop_imag):
    field_real = (win_real * wave_real.astype(jnp.float32) - win_imag * wave_imag.astype(jnp.float32)).astype(jnp.bfloat16)
    field_imag = (win_real * wave_imag.astype(jnp.float32) + win_imag * wave_real.astype(jnp.float32)).astype(jnp.bfloat16)
    out_real, out_imag = apply_both(prop_real, prop_imag, field_real, field_imag)
    return (out_real.astype(jnp.bfloat16), out_imag.astype(jnp.bfloat16))

def modulus(exit_real, exit_imag, amplitude, four_real, four_imag):
    far_real, far_imag = apply_both(four_real, four_imag, exit_real, exit_imag)
    amp = jnp.sqrt(far_real * far_real + far_imag * far_imag + softening)
    ratio = (amp - amplitude.astype(jnp.float32)) / amp
    resid_real = (ratio * far_real).astype(jnp.bfloat16)
    resid_imag = (ratio * far_imag).astype(jnp.bfloat16)
    back_real, back_imag = apply_both(four_real, -four_imag, resid_real, resid_imag)
    return (back_real.astype(jnp.bfloat16), back_imag.astype(jnp.bfloat16))

def backward_slice(win_real, win_imag, grad_real, grad_imag, wave_real, wave_imag, prop_real, prop_imag):
    back_real, back_imag = apply_both(prop_real, -prop_imag, grad_real, grad_imag)
    psi_real = wave_real.astype(jnp.float32)
    psi_imag = wave_imag.astype(jnp.float32)
    contrib_real = back_real * psi_real + back_imag * psi_imag
    contrib_imag = back_imag * psi_real - back_real * psi_imag
    out_real = (back_real * win_real + back_imag * win_imag).astype(jnp.bfloat16)
    out_imag = (back_imag * win_real - back_real * win_imag).astype(jnp.bfloat16)
    return (contrib_real, contrib_imag, out_real, out_imag)

def reference(trans_real, trans_imag, probe_real, probe_imag, offsets, pattern_index, measured):
    prop_real, prop_imag, four_real, four_imag = tables(WIN)

    def one_tile(tile_no):
        first = (tile_no * POS_TILE).astype(jnp.int32)
        offset_sel = lax.dynamic_slice_in_dim(offsets, first, POS_TILE, 1)
        rows_sel = lax.dynamic_slice_in_dim(pattern_index, first, POS_TILE, 0)
        amplitude = jnp.take(measured, rows_sel, axis=0)
        corner = (tile_no * PATCH).astype(jnp.int32)
        patch_real = lax.dynamic_slice_in_dim(trans_real, corner, PATCH, 1)
        patch_imag = lax.dynamic_slice_in_dim(trans_imag, corner, PATCH, 1)
        wave_real = jnp.broadcast_to(probe_real, (POS_TILE, WIN, WIN))
        wave_imag = jnp.broadcast_to(probe_imag, (POS_TILE, WIN, WIN))
        stored = []
        for layer in range(SLICES):
            win_real = windows(patch_real[layer], offset_sel, WIN)
            win_imag = windows(patch_imag[layer], offset_sel, WIN)
            stored.append((wave_real, wave_imag))
            wave_real, wave_imag = forward_slice(win_real, win_imag, wave_real, wave_imag, prop_real, prop_imag)
        grad_real, grad_imag = modulus(wave_real, wave_imag, amplitude, four_real, four_imag)
        real_parts = [None] * SLICES
        imag_parts = [None] * SLICES
        for layer in reversed(range(SLICES)):
            win_real = windows(patch_real[layer], offset_sel, WIN)
            win_imag = windows(patch_imag[layer], offset_sel, WIN)
            contrib_real, contrib_imag, grad_real, grad_imag = backward_slice(win_real, win_imag, grad_real, grad_imag, stored[layer][0], stored[layer][1], prop_real, prop_imag)
            empty = jnp.zeros((PATCH, PATCH), jnp.float32)
            real_parts[layer] = accumulate(empty, contrib_real, offset_sel, WIN)
            imag_parts[layer] = accumulate(empty, contrib_imag, offset_sel, WIN)
        return jnp.stack([jnp.stack(real_parts), jnp.stack(imag_parts)])
    tile_ids = jnp.arange(N_TILE, dtype=jnp.int32)
    result = lax.map(one_tile, tile_ids)
    return jnp.transpose(result, (1, 2, 0, 3, 4)).reshape(2, SLICES, N_TILE * PATCH, PATCH)
```

```python
import functools
import math

import jax
import jax.numpy as jnp
import ml_dtypes
import numpy as np
from jax import lax
from jax.experimental import pallas as pl
from jax.experimental.pallas import tpu as pltpu
from jax.sharding import PartitionSpec as P

fresnel_strength = 9.0
softening = 0.01
LANES = 128


def tables(extent):
    indices = np.arange(extent)
    angles = (indices[:, None] * indices[None, :] % extent) * (2.0 * math.pi / extent)
    wave = np.cos(angles) + 1j * np.sin(angles)
    frequency = np.where(indices < (extent + 1) // 2, indices, indices - extent) / extent
    kernel = np.exp(-1j * fresnel_strength * frequency * frequency)
    prop = (wave * kernel[None, :]) @ wave.conj() / extent
    four = wave.conj() / math.sqrt(extent)
    blocks = []
    for matrix in (prop, four):
        real, imag = matrix.real, matrix.imag
        blocks.append(np.block([[real, -imag], [imag, real]]))
        blocks.append(np.block([[real, imag], [-imag, real]]))
    return [b.astype(np.float32).astype(ml_dtypes.bfloat16) for b in blocks]


def apply_both(left, right, fields):
    extent = fields[0][0].shape[0]
    count = len(fields)
    cat = jnp.concatenate(
        [
            jnp.concatenate([f[0] for f in fields], axis=1),
            jnp.concatenate([f[1] for f in fields], axis=1),
        ],
        axis=0,
    )
    mid = jnp.dot(left, cat, preferred_element_type=jnp.float32).astype(jnp.bfloat16)
    rows = jnp.concatenate(
        [
            jnp.concatenate(
                [
                    mid[:extent, n * extent : (n + 1) * extent],
                    mid[extent:, n * extent : (n + 1) * extent],
                ],
                axis=1,
            )
            for n in range(count)
        ],
        axis=0,
    )
    end = jnp.dot(rows, right, preferred_element_type=jnp.float32)
    return [
        (
            end[n * extent : (n + 1) * extent, :extent],
            end[n * extent : (n + 1) * extent, extent:],
        )
        for n in range(count)
    ]


def kernel(
    tiles,
    slices,
    count,
    chunk,
    off_ref,
    own_ref,
    trr_ref,
    tri_ref,
    pr_ref,
    pi_ref,
    req_ref,
    meas_ref,
    lg_ref,
    rg_ref,
    lf_ref,
    rf_ref,
    out_ref,
    slab,
    tsend,
    trecv,
    rrecv,
    psend,
    pats,
    wins,
    psis,
    far,
    grads,
    pad,
    acc,
    gsend,
    grecv,
    ts_sem,
    tr_sem,
    rs_sem,
    rr_sem,
    ps_sem,
    pr_sem,
    gs_sem,
    gr_sem,
):
    extent = pr_ref.shape[0]
    height = trr_ref.shape[1]
    reach = height - extent
    halves = trr_ref.shape[2] // LANES
    cut = lax.axis_index("cuts")
    tile = lax.axis_index("tile")

    def tile_at(step):
        return {"tile": lax.rem(tile + step, tiles)}

    def cut_at(step):
        return {"cuts": lax.rem(cut + step, slices)}

    barrier = pltpu.get_barrier_semaphore()
    for step in range(1, tiles):
        pl.semaphore_signal(
            barrier, inc=1, device_id=tile_at(step), device_id_type=pl.DeviceIdType.MESH
        )
    for step in range(1, slices):
        pl.semaphore_signal(
            barrier, inc=1, device_id=cut_at(step), device_id_type=pl.DeviceIdType.MESH
        )

    def split_own(plane, ref):
        for half in range(halves):
            block = ref[0, :, half * LANES : (half + 1) * LANES]
            slab[cut, plane, half] = block
            tsend[plane, half] = block.astype(jnp.bfloat16)

    split_own(0, trr_ref)
    split_own(1, tri_ref)
    pl.semaphore_wait(barrier, tiles - 1 + slices - 1)

    def request_copy(step):
        return pltpu.make_async_remote_copy(
            src_ref=req_ref.at[lax.rem(tile + step, tiles)],
            dst_ref=rrecv.at[step],
            send_sem=rs_sem.at[step],
            recv_sem=rr_sem.at[step],
            device_id=tile_at(step),
            device_id_type=pl.DeviceIdType.MESH,
        )

    def slab_copy(step):
        return pltpu.make_async_remote_copy(
            src_ref=tsend,
            dst_ref=trecv.at[step - 1],
            send_sem=ts_sem.at[step - 1],
            recv_sem=tr_sem.at[step - 1],
            device_id=cut_at(step),
            device_id_type=pl.DeviceIdType.MESH,
        )

    def pattern_copy(step):
        return pltpu.make_async_remote_copy(
            src_ref=psend.at[step],
            dst_ref=pats.at[step],
            send_sem=ps_sem.at[step],
            recv_sem=pr_sem.at[step],
            device_id=tile_at(tiles - step),
            device_id_type=pl.DeviceIdType.MESH,
        )

    for step in range(1, tiles):
        request_copy(step).start()
    for step in range(1, slices):
        slab_copy(step).start()

    acc[...] = jnp.zeros_like(acc)
    pad[...] = jnp.zeros_like(pad)
    pats[0] = meas_ref[req_ref[tile][0, 0]]
    for step in range(1, tiles):
        request_copy(step).wait_recv()
        psend[step] = meas_ref[rrecv[step][0, 0]]
        pattern_copy(step).start()

    for step in range(1, slices):
        slab_copy(step).wait_recv()
        slab[lax.rem(cut + slices - step, slices)] = trecv[step - 1].astype(jnp.float32)

    lane = lax.broadcasted_iota(jnp.int32, (extent, LANES), 1)

    def window(layer, plane, row, col):
        low = slab[layer, plane, 0, pl.ds(row, extent), :]
        high = slab[layer, plane, 1, pl.ds(row, extent), :]
        return pltpu.roll(
            jnp.where(lane >= col, low, high), lax.rem(2 * LANES - col, LANES), axis=1
        )

    def descend(item, _):
        base = item * chunk
        probe = (pr_ref[...], pi_ref[...])
        waves = [probe] * chunk
        for layer in range(slices):
            fields = []
            for n in range(chunk):
                row, col = off_ref[0, base + n], off_ref[1, base + n]
                win_real = window(layer, 0, row, col)
                win_imag = window(layer, 1, row, col)
                if layer > 0:
                    wins[layer - 1, base + n, 0] = win_real
                    wins[layer - 1, base + n, 1] = win_imag
                    psis[layer - 1, base + n, 0] = waves[n][0]
                    psis[layer - 1, base + n, 1] = waves[n][1]
                wave_real = waves[n][0].astype(jnp.float32)
                wave_imag = waves[n][1].astype(jnp.float32)
                fields.append(
                    (
                        (win_real * wave_real - win_imag * wave_imag).astype(jnp.bfloat16),
                        (win_real * wave_imag + win_imag * wave_real).astype(jnp.bfloat16),
                    )
                )
            ends = apply_both(lg_ref[...], rg_ref[...], fields)
            waves = [(e[0].astype(jnp.bfloat16), e[1].astype(jnp.bfloat16)) for e in ends]
        ends = apply_both(lf_ref[...], rf_ref[...], waves)
        for n in range(chunk):
            far[base + n, 0] = ends[n][0]
            far[base + n, 1] = ends[n][1]
        return 0

    lax.fori_loop(0, count // chunk, descend, 0)

    for step in range(1, tiles):
        pattern_copy(step).wait_recv()

    def seeds(base):
        fields = []
        for n in range(chunk):
            owner = own_ref[0, base + n]
            amplitude = pats[lax.rem(owner - tile + tiles, tiles)].astype(jnp.float32)
            far_real = far[base + n, 0]
            far_imag = far[base + n, 1]
            inverse = lax.rsqrt(far_real * far_real + far_imag * far_imag + softening)
            ratio = 1.0 - amplitude * inverse
            fields.append(
                (
                    (ratio * far_real).astype(jnp.bfloat16),
                    (ratio * far_imag).astype(jnp.bfloat16),
                )
            )
        ends = apply_both(rf_ref[...], lf_ref[...], fields)
        return [(e[0].astype(jnp.bfloat16), e[1].astype(jnp.bfloat16)) for e in ends]

    def grad_copy(layer):
        step = lax.rem(layer - cut + slices, slices)
        return pltpu.make_async_remote_copy(
            src_ref=gsend.at[layer],
            dst_ref=grecv.at[step - 1],
            send_sem=gs_sem.at[layer],
            recv_sem=gr_sem.at[step - 1],
            device_id={"cuts": layer},
            device_id_type=pl.DeviceIdType.MESH,
        )

    for layer in reversed(range(slices)):

        def ascend(item, _):
            base = item * chunk
            if layer == slices - 1:
                fields = seeds(base)
            else:
                fields = [(grads[base + n, 0], grads[base + n, 1]) for n in range(chunk)]
            ends = apply_both(rg_ref[...], lg_ref[...], fields)
            for n in range(chunk):
                back_real, back_imag = ends[n]
                col = off_ref[1, base + n]
                if layer > 0:
                    psi_real = psis[layer - 1, base + n, 0].astype(jnp.float32)
                    psi_imag = psis[layer - 1, base + n, 1].astype(jnp.float32)
                    win_real = wins[layer - 1, base + n, 0]
                    win_imag = wins[layer - 1, base + n, 1]
                    grads[base + n, 0] = (back_real * win_real + back_imag * win_imag).astype(
                        jnp.bfloat16
                    )
                    grads[base + n, 1] = (back_imag * win_real - back_real * win_imag).astype(
                        jnp.bfloat16
                    )
                else:
                    psi_real = pr_ref[...].astype(jnp.float32)
                    psi_imag = pi_ref[...].astype(jnp.float32)
                terms = (
                    back_real * psi_real + back_imag * psi_imag,
                    back_imag * psi_real - back_real * psi_imag,
                )
                for plane in range(2):
                    rolled = pltpu.roll(terms[plane], lax.rem(col, LANES), axis=1)
                    pad[n, plane, 0, reach : reach + extent] = jnp.where(lane >= col, rolled, 0.0)
                    pad[n, plane, 1, reach : reach + extent] = jnp.where(lane < col, rolled, 0.0)
            for plane in range(2):
                for half in range(2):
                    total = acc[layer, plane, half]
                    for n in range(chunk):
                        start = reach - off_ref[0, base + n]
                        total = total + pad[n, plane, half, pl.ds(start, height), :]
                    acc[layer, plane, half] = total
            return 0

        lax.fori_loop(0, count // chunk, ascend, 0)

        @pl.when(cut != layer)
        def _():
            gsend[layer] = acc[layer].astype(jnp.bfloat16)
            grad_copy(layer).start()

    for step in range(1, slices):
        pltpu.make_async_remote_copy(
            src_ref=gsend.at[0],
            dst_ref=grecv.at[step - 1],
            send_sem=gs_sem.at[0],
            recv_sem=gr_sem.at[step - 1],
            device_id=cut_at(step),
            device_id_type=pl.DeviceIdType.MESH,
        ).wait_recv()
    for plane in range(2):
        for half in range(2):
            total = acc[cut, plane, half]
            for step in range(1, slices):
                total = total + grecv[step - 1, plane, half].astype(jnp.float32)
            out_ref[plane, 0, :, half * LANES : (half + 1) * LANES] = total

    for step in range(1, tiles):
        request_copy(step).wait_send()
        pattern_copy(step).wait_send()
    for step in range(1, slices):
        slab_copy(step).wait_send()
    for layer in range(slices):

        @pl.when(cut != layer)
        def _():
            grad_copy(layer).wait_send()


def local(trans_real, trans_imag, probe_real, probe_imag, offsets, pattern_index, measured):
    extent = probe_real.shape[-1]
    positions = pattern_index.shape[0]
    tiles = lax.axis_size("tile")
    slices = lax.axis_size("cuts")
    cut = lax.axis_index("cuts")
    height, width = trans_real.shape[1:]
    assert extent == LANES and width == 2 * LANES and trans_real.shape[0] == 1
    assert positions % slices == 0
    assert (positions + tiles - 1) // tiles <= slices
    count = positions // slices
    chunk = math.gcd(count, 4)

    owners = pattern_index // positions
    slots = pattern_index % positions
    order_key = owners * positions + jnp.arange(positions, dtype=jnp.int32)
    ordinal = jnp.sum((order_key[None, :] < order_key[:, None]).astype(jnp.int32), axis=1)
    places = jnp.arange(count, dtype=jnp.int32) * slices + cut
    hit = (places[:, None] == ordinal[None, :]).astype(jnp.int32)
    off_mine = jnp.sum(hit[None] * offsets[:, None, :], axis=2)
    own_mine = jnp.sum(hit * owners[None, :], axis=1)[None]
    wanted = (owners[None, :] == jnp.arange(tiles, dtype=jnp.int32)[:, None]) & (
        lax.rem(ordinal, slices) == cut
    )[None, :]
    request = jnp.sum(jnp.where(wanted, slots[None, :], 0), axis=1)
    request = jnp.broadcast_to(request[:, None, None], (tiles, 1, LANES))

    blocks = [jnp.asarray(b) for b in tables(extent)]
    others = max(slices - 1, 1)
    bf16, f32 = jnp.bfloat16, jnp.float32
    vmem = pl.BlockSpec(memory_space=pltpu.VMEM)
    smem = pl.BlockSpec(memory_space=pltpu.SMEM)
    dma = pltpu.SemaphoreType.DMA
    return pl.pallas_call(
        functools.partial(kernel, tiles, slices, count, chunk),
        out_shape=jax.ShapeDtypeStruct((2, 1, height, width), f32),
        in_specs=[smem, smem] + [vmem] * 10,
        out_specs=vmem,
        scratch_shapes=[
            pltpu.VMEM((slices, 2, 2, height, LANES), f32),
            pltpu.VMEM((2, 2, height, LANES), bf16),
            pltpu.VMEM((others, 2, 2, height, LANES), bf16),
            pltpu.VMEM((tiles, 1, LANES), jnp.int32),
            pltpu.VMEM((tiles, extent, extent), bf16),
            pltpu.VMEM((tiles, extent, extent), bf16),
            pltpu.VMEM((others, count, 2, extent, extent), f32),
            pltpu.VMEM((others, count, 2, extent, extent), bf16),
            pltpu.VMEM((count, 2, extent, extent), f32),
            pltpu.VMEM((count, 2, extent, extent), bf16),
            pltpu.VMEM((chunk, 2, 2, 2 * height - extent, LANES), f32),
            pltpu.VMEM((slices, 2, 2, height, LANES), f32),
            pltpu.VMEM((slices, 2, 2, height, LANES), bf16),
            pltpu.VMEM((others, 2, 2, height, LANES), bf16),
            dma((others,)),
            dma((others,)),
            dma((tiles,)),
            dma((tiles,)),
            dma((tiles,)),
            dma((tiles,)),
            dma((slices,)),
            dma((others,)),
        ],
        compiler_params=pltpu.CompilerParams(
            collective_id=0, has_side_effects=True, vmem_limit_bytes=56 * 1024 * 1024
        ),
    )(off_mine, own_mine, trans_real, trans_imag, probe_real, probe_imag, request, measured, *blocks)


def solution(mesh):
    return jax.shard_map(
        local,
        mesh=mesh,
        in_specs=(
            P("cuts", "tile", None),
            P("cuts", "tile", None),
            P(),
            P(),
            P(None, "tile"),
            P("tile"),
            P("tile", None, None),
        ),
        out_specs=P(None, "cuts", "tile", None),
        check_vma=False,
    )
```

```python
import functools
import math

import jax
import jax.numpy as jnp
import ml_dtypes
import numpy as np
from jax import lax
from jax.experimental import pallas as pl
from jax.experimental.pallas import tpu as pltpu
from jax.sharding import PartitionSpec as P

fresnel_strength = 9.0
softening = 0.01
LANES = 128


def tables(extent):
    indices = np.arange(extent)
    angles = (indices[:, None] * indices[None, :] % extent) * (2.0 * math.pi / extent)
    wave = np.cos(angles) + 1j * np.sin(angles)
    frequency = np.where(indices < (extent + 1) // 2, indices, indices - extent) / extent
    kernel = np.exp(-1j * fresnel_strength * frequency * frequency)
    prop = (wave * kernel[None, :]) @ wave.conj() / extent
    four = wave.conj() / math.sqrt(extent)
    blocks = []
    for matrix in (prop, four):
        real, imag = matrix.real, matrix.imag
        blocks.append(np.block([[real, -imag], [imag, real]]))
        blocks.append(np.block([[real, imag], [-imag, real]]))
    return [b.astype(np.float32).astype(ml_dtypes.bfloat16) for b in blocks]


def apply_both(left, right, fields):
    extent = fields[0][0].shape[0]
    count = len(fields)
    cat = jnp.concatenate(
        [
            jnp.concatenate([f[0] for f in fields], axis=1),
            jnp.concatenate([f[1] for f in fields], axis=1),
        ],
        axis=0,
    )
    mid = jnp.dot(left, cat, preferred_element_type=jnp.float32).astype(jnp.bfloat16)
    rows = jnp.concatenate(
        [
            jnp.concatenate(
                [
                    mid[:extent, n * extent : (n + 1) * extent],
                    mid[extent:, n * extent : (n + 1) * extent],
                ],
                axis=1,
            )
            for n in range(count)
        ],
        axis=0,
    )
    end = jnp.dot(rows, right, preferred_element_type=jnp.float32)
    return [
        (
            end[n * extent : (n + 1) * extent, :extent],
            end[n * extent : (n + 1) * extent, extent:],
        )
        for n in range(count)
    ]


def exclusive_or(first, second, size):
    result, unit = 0, 1
    while unit < size:
        one, two = first // unit % 2, second // unit % 2
        result = result + (one + two - 2 * one * two) * unit
        unit *= 2
    return result


def kernel(
    tiles,
    slices,
    count,
    chunk,
    exact,
    off_ref,
    index_ref,
    pr_ref,
    pi_ref,
    trr_ref,
    tri_ref,
    meas_hbm,
    table_hbm,
    own_out,
    recv_out,
    meas,
    table,
    place,
    source,
    qsend,
    slab,
    tsend,
    trecv,
    rrecv,
    psend,
    pats,
    wins,
    psis,
    far,
    pad,
    acc,
    gsend,
    in_sem,
    ts_sem,
    tr_sem,
    rs_sem,
    rr_sem,
    ps_sem,
    pr_sem,
    gs_sem,
    gr_sem,
    own_sem,
):
    extent = pr_ref.shape[0]
    height = trr_ref.shape[1]
    positions = index_ref.shape[1]
    reach = height - extent
    cut = lax.axis_index("cuts")
    tile = lax.axis_index("tile")
    mesh_ids = pl.DeviceIdType.MESH

    def peer(step):
        return exclusive_or(tile, step, tiles)

    def cut_at(step):
        return {"cuts": lax.rem(cut + step, slices)}

    barrier = pltpu.get_barrier_semaphore()
    near = list(range(1, tiles // 2))
    order = []
    for step in range(tiles // 2, tiles):
        order.append(step)
        if near:
            order.append(near.pop(0))
    for step in order:
        pl.semaphore_signal(
            barrier, inc=1, device_id={"tile": peer(step)}, device_id_type=mesh_ids
        )
    for step in range(1, slices):
        pl.semaphore_signal(barrier, inc=1, device_id=cut_at(step), device_id_type=mesh_ids)

    slab_in = [
        pltpu.make_async_copy(
            ref.at[0, :, pl.ds(half * LANES, LANES)],
            slab.at[cut, plane, half],
            in_sem.at[2 + 2 * plane + half],
        )
        for plane, ref in enumerate((trr_ref, tri_ref))
        for half in range(2)
    ]
    meas_in = pltpu.make_async_copy(meas_hbm, meas, in_sem.at[0])
    table_in = pltpu.make_async_copy(table_hbm, table, in_sem.at[1])
    for copy in slab_in:
        copy.start()
    meas_in.start()
    table_in.start()

    wanted = index_ref[...]
    lanes = lax.broadcasted_iota(jnp.int32, (1, positions), 1)
    key_row = jnp.broadcast_to(wanted // positions * positions + lanes, (positions, positions))
    diagonal = lax.broadcasted_iota(jnp.int32, (positions, positions), 0) == (
        lax.broadcasted_iota(jnp.int32, (positions, positions), 1)
    )
    key_col = jnp.sum(jnp.where(diagonal, key_row, 0), axis=1, keepdims=True)
    ordinal = jnp.sum(jnp.where(key_col < key_row, 1, 0), axis=0, keepdims=True)
    asked = jnp.where(lax.rem(ordinal, slices) == cut, wanted, -1)
    qsend[...] = jnp.full_like(qsend, -1)
    qsend[:, :positions] = asked

    for copy in slab_in:
        copy.wait()
    for plane in range(2):
        for half in range(2):
            tsend[plane, half] = slab[cut, plane, half].astype(jnp.bfloat16)
    pl.semaphore_wait(barrier, tiles - 1 + slices - 1)

    def request_copy(step):
        return pltpu.make_async_remote_copy(
            src_ref=qsend,
            dst_ref=rrecv.at[step],
            send_sem=rs_sem.at[step],
            recv_sem=rr_sem.at[step],
            device_id={"tile": peer(step)},
            device_id_type=mesh_ids,
        )

    def slab_copy(step):
        return pltpu.make_async_remote_copy(
            src_ref=tsend,
            dst_ref=trecv.at[step - 1],
            send_sem=ts_sem.at[step - 1],
            recv_sem=tr_sem.at[step - 1],
            device_id=cut_at(step),
            device_id_type=mesh_ids,
        )

    def pattern_copy(step):
        return pltpu.make_async_remote_copy(
            src_ref=psend.at[step],
            dst_ref=pats.at[step],
            send_sem=ps_sem.at[step],
            recv_sem=pr_sem.at[step],
            device_id={"tile": peer(step)},
            device_id_type=mesh_ids,
        )

    def pattern_for(row):
        slot = row - tile * positions
        slot = jnp.max(jnp.where((slot >= 0) & (slot < positions), slot, 0))
        return meas[slot]

    for step in order:
        request_copy(step).start()
    for step in range(1, slices):
        slab_copy(step).start()
    for item in range(count):
        owner = peer(item) if exact else item
        match = ordinal == owner * slices + cut
        place[item] = jnp.max(jnp.where(match, lanes, 0))
        if not exact:
            owner = jnp.max(jnp.where(match, wanted, 0)) // positions
            source[item] = exclusive_or(tile, owner, tiles)
    meas_in.wait()
    for step in order:
        request_copy(step).wait_recv()
        psend[step] = pattern_for(rrecv[step])
        pattern_copy(step).start()
    pats[0] = pattern_for(qsend[...])
    acc[...] = jnp.zeros_like(acc)
    pad[...] = jnp.zeros_like(pad)
    table_in.wait()

    for step in range(1, slices):
        slab_copy(step).wait_recv()
        slab[lax.rem(cut + slices - step, slices)] = trecv[step - 1].astype(jnp.float32)

    lane = lax.broadcasted_iota(jnp.int32, (extent, LANES), 1)

    def window(layer, plane, row, col):
        low = slab[layer, plane, 0, pl.ds(row, extent), :]
        high = slab[layer, plane, 1, pl.ds(row, extent), :]
        return pltpu.roll(
            jnp.where(lane >= col, low, high), lax.rem(2 * LANES - col, LANES), axis=1
        )

    def descend(item, _):
        base = item * chunk
        waves = [(pr_ref[...], pi_ref[...])] * chunk
        for layer in range(slices):
            fields = []
            for n in range(chunk):
                at = place[base + n]
                row, col = off_ref[0, at], off_ref[1, at]
                win_real = window(layer, 0, row, col)
                win_imag = window(layer, 1, row, col)
                if layer > 0:
                    wins[layer - 1, base + n, 0] = win_real
                    wins[layer - 1, base + n, 1] = win_imag
                    psis[layer - 1, base + n, 0] = waves[n][0]
                    psis[layer - 1, base + n, 1] = waves[n][1]
                wave_real = waves[n][0].astype(jnp.float32)
                wave_imag = waves[n][1].astype(jnp.float32)
                fields.append(
                    (
                        (win_real * wave_real - win_imag * wave_imag).astype(jnp.bfloat16),
                        (win_real * wave_imag + win_imag * wave_real).astype(jnp.bfloat16),
                    )
                )
            ends = apply_both(table[0], table[1], fields)
            waves = [(e[0].astype(jnp.bfloat16), e[1].astype(jnp.bfloat16)) for e in ends]
        ends = apply_both(table[2], table[3], waves)
        for n in range(chunk):
            far[base + n, 0] = ends[n][0]
            far[base + n, 1] = ends[n][1]
        return 0

    lax.fori_loop(0, count // chunk, descend, 0)

    if not exact:
        for step in order:
            pattern_copy(step).wait_recv()

    def seeds(base):
        fields = []
        for n in range(chunk):
            at = base + n if exact else source[base + n]
            amplitude = pats[at].astype(jnp.float32)
            far_real = far[base + n, 0]
            far_imag = far[base + n, 1]
            inverse = lax.rsqrt(far_real * far_real + far_imag * far_imag + softening)
            ratio = 1.0 - amplitude * inverse
            fields.append(
                (
                    (ratio * far_real).astype(jnp.bfloat16),
                    (ratio * far_imag).astype(jnp.bfloat16),
                )
            )
        ends = apply_both(table[3], table[2], fields)
        return [(e[0].astype(jnp.bfloat16), e[1].astype(jnp.bfloat16)) for e in ends]

    def grad_copy(layer, step, plane, half, target):
        return pltpu.make_async_remote_copy(
            src_ref=gsend.at[layer, plane, half],
            dst_ref=recv_out.at[step - 1, plane, :, pl.ds(half * LANES, LANES)],
            send_sem=gs_sem.at[layer, plane, half],
            recv_sem=gr_sem.at[step - 1, plane, half],
            device_id={"cuts": target},
            device_id_type=mesh_ids,
        )

    def grad_to(layer, plane, half):
        return grad_copy(layer, lax.rem(layer - cut + slices, slices), plane, half, layer)

    def own_copy(layer, plane, half):
        return pltpu.make_async_copy(
            acc.at[layer, plane, half],
            own_out.at[plane, 0, :, pl.ds(half * LANES, LANES)],
            own_sem.at[plane, half],
        )

    chunks = count // chunk

    def ascend(item, _):
        base = item * chunk
        if exact:
            for n in range(chunk):

                @pl.when(base + n > 0)
                def _():
                    pattern_copy(base + n).wait_recv()

        fields = seeds(base)
        for layer in reversed(range(slices)):
            ends = apply_both(table[1], table[0], fields)
            fields = []
            for n in range(chunk):
                back_real, back_imag = ends[n]
                col = off_ref[1, place[base + n]]
                if layer > 0:
                    psi_real = psis[layer - 1, base + n, 0].astype(jnp.float32)
                    psi_imag = psis[layer - 1, base + n, 1].astype(jnp.float32)
                    win_real = wins[layer - 1, base + n, 0]
                    win_imag = wins[layer - 1, base + n, 1]
                    fields.append(
                        (
                            (back_real * win_real + back_imag * win_imag).astype(jnp.bfloat16),
                            (back_imag * win_real - back_real * win_imag).astype(jnp.bfloat16),
                        )
                    )
                else:
                    psi_real = pr_ref[...].astype(jnp.float32)
                    psi_imag = pi_ref[...].astype(jnp.float32)
                terms = (
                    back_real * psi_real + back_imag * psi_imag,
                    back_imag * psi_real - back_real * psi_imag,
                )
                for plane in range(2):
                    rolled = pltpu.roll(terms[plane], lax.rem(col, LANES), axis=1)
                    pad[n, plane, 0, reach : reach + extent] = jnp.where(lane >= col, rolled, 0.0)
                    pad[n, plane, 1, reach : reach + extent] = jnp.where(lane < col, rolled, 0.0)
            for plane in range(2):
                for half in range(2):
                    total = acc[layer, plane, half]
                    for n in range(chunk):
                        start = reach - off_ref[0, place[base + n]]
                        total = total + pad[n, plane, half, pl.ds(start, height), :]
                    acc[layer, plane, half] = total

                    @pl.when((item == chunks - 1) & (cut != layer))
                    def _():
                        gsend[layer, plane, half] = acc[layer, plane, half].astype(jnp.bfloat16)
                        grad_to(layer, plane, half).start()

                    @pl.when((item == chunks - 1) & (cut == layer))
                    def _():
                        own_copy(layer, plane, half).start()

        return 0

    lax.fori_loop(0, chunks, ascend, 0)

    for step in order:
        request_copy(step).wait_send()
        pattern_copy(step).wait_send()
    for step in range(1, slices):
        slab_copy(step).wait_send()
    for plane in range(2):
        for half in range(2):
            own_copy(cut, plane, half).wait()
            for layer in range(slices):

                @pl.when(cut != layer)
                def _():
                    grad_to(layer, plane, half).wait_send()

            for step in range(1, slices):
                grad_copy(0, step, plane, half, lax.rem(cut + step, slices)).wait_recv()


def local(trans_real, trans_imag, probe_real, probe_imag, offsets, pattern_index, measured):
    extent = probe_real.shape[-1]
    positions = pattern_index.shape[0]
    tiles = lax.axis_size("tile")
    slices = lax.axis_size("cuts")
    height, width = trans_real.shape[1:]
    assert extent == LANES and width == 2 * LANES and trans_real.shape[0] == 1
    assert positions % slices == 0 and positions <= LANES
    assert tiles & (tiles - 1) == 0
    assert (positions + tiles - 1) // tiles <= slices
    count = positions // slices
    chunk = math.gcd(count, 4)
    exact = count == tiles

    others = slices - 1
    bf16, f32 = jnp.bfloat16, jnp.float32
    vmem = pl.BlockSpec(memory_space=pltpu.VMEM)
    smem = pl.BlockSpec(memory_space=pltpu.SMEM)
    hbm = pl.BlockSpec(memory_space=pl.ANY)
    dma = pltpu.SemaphoreType.DMA
    own, received = pl.pallas_call(
        functools.partial(kernel, tiles, slices, count, chunk, exact),
        out_shape=(
            jax.ShapeDtypeStruct((2, 1, height, width), f32),
            jax.ShapeDtypeStruct((others, 2, height, width), bf16),
        ),
        in_specs=[smem, vmem, vmem, vmem, hbm, hbm, hbm, hbm],
        out_specs=(hbm, hbm),
        scratch_shapes=[
            pltpu.VMEM(measured.shape, bf16),
            pltpu.VMEM((4, 2 * extent, 2 * extent), bf16),
            pltpu.SMEM((count,), jnp.int32),
            pltpu.SMEM((count,), jnp.int32),
            pltpu.VMEM((1, LANES), jnp.int32),
            pltpu.VMEM((slices, 2, 2, height, LANES), f32),
            pltpu.VMEM((2, 2, height, LANES), bf16),
            pltpu.VMEM((others, 2, 2, height, LANES), bf16),
            pltpu.VMEM((tiles, 1, LANES), jnp.int32),
            pltpu.VMEM((tiles, extent, extent), bf16),
            pltpu.VMEM((tiles, extent, extent), bf16),
            pltpu.VMEM((others, count, 2, extent, extent), f32),
            pltpu.VMEM((others, count, 2, extent, extent), bf16),
            pltpu.VMEM((count, 2, extent, extent), f32),
            pltpu.VMEM((chunk, 2, 2, 2 * height - extent, LANES), f32),
            pltpu.VMEM((slices, 2, 2, height, LANES), f32),
            pltpu.VMEM((slices, 2, 2, height, LANES), bf16),
            dma((6,)),
            dma((others,)),
            dma((others,)),
            dma((tiles,)),
            dma((tiles,)),
            dma((tiles,)),
            dma((tiles,)),
            dma((slices, 2, 2)),
            dma((others, 2, 2)),
            dma((2, 2)),
        ],
        compiler_params=pltpu.CompilerParams(
            collective_id=0, has_side_effects=True, vmem_limit_bytes=56 * 1024 * 1024
        ),
    )(
        offsets,
        pattern_index[None],
        probe_real,
        probe_imag,
        trans_real,
        trans_imag,
        measured,
        jnp.asarray(np.stack(tables(extent))),
    )
    return own + jnp.sum(received.astype(f32), axis=0)[:, None]


def solution(mesh):
    return jax.shard_map(
        local,
        mesh=mesh,
        in_specs=(
            P("cuts", "tile", None),
            P("cuts", "tile", None),
            P(),
            P(),
            P(None, "tile"),
            P("tile"),
            P("tile", None, None),
        ),
        out_specs=P(None, "cuts", "tile", None),
        check_vma=False,
    )
```

```python
import functools
import math

import jax
import jax.numpy as jnp
import ml_dtypes
import numpy as np
from jax import lax
from jax.experimental import pallas as pl
from jax.experimental.pallas import tpu as pltpu
from jax.sharding import PartitionSpec as P

fresnel_strength = 9.0
softening = 0.01
LANES = 128


def tables(extent):
    indices = np.arange(extent)
    angles = (indices[:, None] * indices[None, :] % extent) * (2.0 * math.pi / extent)
    wave = np.cos(angles) + 1j * np.sin(angles)
    frequency = np.where(indices < (extent + 1) // 2, indices, indices - extent) / extent
    kernel = np.exp(-1j * fresnel_strength * frequency * frequency)
    prop = (wave * kernel[None, :]) @ wave.conj() / extent
    four = wave.conj() / math.sqrt(extent)
    blocks = []
    for matrix in (prop, four):
        real, imag = matrix.real, matrix.imag
        blocks.append(np.block([[real, -imag], [imag, real]]))
        blocks.append(np.block([[real, imag], [-imag, real]]))
    return [b.astype(np.float32).astype(ml_dtypes.bfloat16) for b in blocks]


def apply_both(left, right, fields):
    extent = fields[0][0].shape[0]
    count = len(fields)
    cat = jnp.concatenate(
        [
            jnp.concatenate([f[0] for f in fields], axis=1),
            jnp.concatenate([f[1] for f in fields], axis=1),
        ],
        axis=0,
    )
    mid = jnp.dot(left, cat, preferred_element_type=jnp.float32).astype(jnp.bfloat16)
    rows = jnp.concatenate(
        [
            jnp.concatenate(
                [
                    mid[:extent, n * extent : (n + 1) * extent],
                    mid[extent:, n * extent : (n + 1) * extent],
                ],
                axis=1,
            )
            for n in range(count)
        ],
        axis=0,
    )
    end = jnp.dot(rows, right, preferred_element_type=jnp.float32)
    return [
        (
            end[n * extent : (n + 1) * extent, :extent],
            end[n * extent : (n + 1) * extent, extent:],
        )
        for n in range(count)
    ]


def exclusive_or(first, second, size):
    result, unit = 0, 1
    while unit < size:
        one, two = first // unit % 2, second // unit % 2
        result = result + (one + two - 2 * one * two) * unit
        unit *= 2
    return result


def kernel(
    tiles,
    slices,
    count,
    chunk,
    exact,
    off_ref,
    index_ref,
    pr_ref,
    pi_ref,
    trr_ref,
    tri_ref,
    meas_hbm,
    table_hbm,
    own_out,
    recv_out,
    meas,
    table,
    place,
    source,
    qsend,
    slab,
    tsend,
    trecv,
    rrecv,
    psend,
    pats,
    wins,
    psis,
    far,
    pad,
    acc,
    gsend,
    in_sem,
    ts_sem,
    tr_sem,
    rs_sem,
    rr_sem,
    ps_sem,
    pr_sem,
    gs_sem,
    gr_sem,
    own_sem,
):
    extent = pr_ref.shape[0]
    height = trr_ref.shape[1]
    positions = index_ref.shape[1]
    reach = height - extent
    cut = lax.axis_index("cuts")
    tile = lax.axis_index("tile")
    mesh_ids = pl.DeviceIdType.MESH

    def peer(step):
        return exclusive_or(tile, step, tiles)

    def cut_at(step):
        return {"cuts": lax.rem(cut + step, slices)}

    barrier = pltpu.get_barrier_semaphore()
    near = list(range(1, tiles // 2))
    order = []
    for step in range(tiles // 2, tiles):
        order.append(step)
        if near:
            order.append(near.pop(0))
    for step in order:
        pl.semaphore_signal(
            barrier, inc=1, device_id={"tile": peer(step)}, device_id_type=mesh_ids
        )
    for step in range(1, slices):
        pl.semaphore_signal(barrier, inc=1, device_id=cut_at(step), device_id_type=mesh_ids)

    slab_in = [
        pltpu.make_async_copy(
            ref.at[0, :, pl.ds(half * LANES, LANES)],
            slab.at[cut, plane, half],
            in_sem.at[2 + 2 * plane + half],
        )
        for plane, ref in enumerate((trr_ref, tri_ref))
        for half in range(2)
    ]
    meas_in = pltpu.make_async_copy(meas_hbm, meas, in_sem.at[0])
    table_in = pltpu.make_async_copy(table_hbm, table, in_sem.at[1])
    for copy in slab_in:
        copy.start()
    meas_in.start()
    table_in.start()

    wanted = index_ref[...]
    lanes = lax.broadcasted_iota(jnp.int32, (1, positions), 1)
    key_row = jnp.broadcast_to(wanted // positions * positions + lanes, (positions, positions))
    diagonal = lax.broadcasted_iota(jnp.int32, (positions, positions), 0) == (
        lax.broadcasted_iota(jnp.int32, (positions, positions), 1)
    )
    key_col = jnp.sum(jnp.where(diagonal, key_row, 0), axis=1, keepdims=True)
    ordinal = jnp.sum(jnp.where(key_col < key_row, 1, 0), axis=0, keepdims=True)
    asked = jnp.where(lax.rem(ordinal, slices) == cut, wanted, -1)
    qsend[...] = jnp.full_like(qsend, -1)
    qsend[:, :positions] = asked

    for copy in slab_in:
        copy.wait()
    for plane in range(2):
        for half in range(2):
            tsend[plane, half] = slab[cut, plane, half].astype(jnp.bfloat16)
    pl.semaphore_wait(barrier, tiles - 1 + slices - 1)

    def request_copy(step):
        return pltpu.make_async_remote_copy(
            src_ref=qsend,
            dst_ref=rrecv.at[step],
            send_sem=rs_sem.at[step],
            recv_sem=rr_sem.at[step],
            device_id={"tile": peer(step)},
            device_id_type=mesh_ids,
        )

    def slab_copy(step):
        return pltpu.make_async_remote_copy(
            src_ref=tsend,
            dst_ref=trecv.at[step - 1],
            send_sem=ts_sem.at[step - 1],
            recv_sem=tr_sem.at[step - 1],
            device_id=cut_at(step),
            device_id_type=mesh_ids,
        )

    def pattern_copy(step):
        return pltpu.make_async_remote_copy(
            src_ref=psend.at[step],
            dst_ref=pats.at[step],
            send_sem=ps_sem.at[step],
            recv_sem=pr_sem.at[step],
            device_id={"tile": peer(step)},
            device_id_type=mesh_ids,
        )

    def pattern_for(row):
        slot = row - tile * positions
        slot = jnp.max(jnp.where((slot >= 0) & (slot < positions), slot, 0))
        return meas[slot]

    for step in order:
        request_copy(step).start()
    for step in range(1, slices):
        slab_copy(step).start()
    for item in range(count):
        owner = peer(item) if exact else item
        match = ordinal == owner * slices + cut
        place[item] = jnp.max(jnp.where(match, lanes, 0))
        if not exact:
            owner = jnp.max(jnp.where(match, wanted, 0)) // positions
            source[item] = exclusive_or(tile, owner, tiles)
    meas_in.wait()
    for step in order:
        request_copy(step).wait_recv()
        psend[step] = pattern_for(rrecv[step])
        pattern_copy(step).start()
    pats[0] = pattern_for(qsend[...])
    acc[...] = jnp.zeros_like(acc)
    pad[...] = jnp.zeros_like(pad)
    table_in.wait()

    for step in range(1, slices):
        slab_copy(step).wait_recv()
        slab[lax.rem(cut + slices - step, slices)] = trecv[step - 1].astype(jnp.float32)

    lane = lax.broadcasted_iota(jnp.int32, (extent, LANES), 1)

    def window(layer, plane, row, col):
        low = slab[layer, plane, 0, pl.ds(row, extent), :]
        high = slab[layer, plane, 1, pl.ds(row, extent), :]
        return pltpu.roll(
            jnp.where(lane >= col, low, high), lax.rem(2 * LANES - col, LANES), axis=1
        )

    wide = math.gcd(count, 8)

    def descend(item, _):
        base = item * wide
        waves = [(pr_ref[...], pi_ref[...])] * wide
        for layer in range(slices):
            fields = []
            for n in range(wide):
                at = place[base + n]
                row, col = off_ref[0, at], off_ref[1, at]
                win_real = window(layer, 0, row, col)
                win_imag = window(layer, 1, row, col)
                if layer > 0:
                    wins[layer - 1, base + n, 0] = win_real
                    wins[layer - 1, base + n, 1] = win_imag
                    psis[layer - 1, base + n, 0] = waves[n][0]
                    psis[layer - 1, base + n, 1] = waves[n][1]
                wave_real = waves[n][0].astype(jnp.float32)
                wave_imag = waves[n][1].astype(jnp.float32)
                fields.append(
                    (
                        (win_real * wave_real - win_imag * wave_imag).astype(jnp.bfloat16),
                        (win_real * wave_imag + win_imag * wave_real).astype(jnp.bfloat16),
                    )
                )
            ends = apply_both(table[0], table[1], fields)
            waves = [(e[0].astype(jnp.bfloat16), e[1].astype(jnp.bfloat16)) for e in ends]
        ends = apply_both(table[2], table[3], waves)
        for n in range(wide):
            far[base + n, 0] = ends[n][0]
            far[base + n, 1] = ends[n][1]
        return 0

    lax.fori_loop(0, count // wide, descend, 0)

    if not exact:
        for step in order:
            pattern_copy(step).wait_recv()

    def seeds(base):
        fields = []
        for n in range(chunk):
            at = base + n if exact else source[base + n]
            amplitude = pats[at].astype(jnp.float32)
            far_real = far[base + n, 0]
            far_imag = far[base + n, 1]
            inverse = lax.rsqrt(far_real * far_real + far_imag * far_imag + softening)
            ratio = 1.0 - amplitude * inverse
            fields.append(
                (
                    (ratio * far_real).astype(jnp.bfloat16),
                    (ratio * far_imag).astype(jnp.bfloat16),
                )
            )
        ends = apply_both(table[3], table[2], fields)
        return [(e[0].astype(jnp.bfloat16), e[1].astype(jnp.bfloat16)) for e in ends]

    def grad_copy(layer, step, plane, half, target):
        return pltpu.make_async_remote_copy(
            src_ref=gsend.at[layer, plane, half],
            dst_ref=recv_out.at[step - 1, plane, :, pl.ds(half * LANES, LANES)],
            send_sem=gs_sem.at[layer, plane, half],
            recv_sem=gr_sem.at[step - 1, plane, half],
            device_id={"cuts": target},
            device_id_type=mesh_ids,
        )

    def grad_to(layer, plane, half):
        return grad_copy(layer, lax.rem(layer - cut + slices, slices), plane, half, layer)

    def own_copy(layer, plane, half):
        return pltpu.make_async_copy(
            acc.at[layer, plane, half],
            own_out.at[plane, 0, :, pl.ds(half * LANES, LANES)],
            own_sem.at[plane, half],
        )

    chunks = count // chunk

    def ascend(item, _):
        base = item * chunk
        if exact:
            for n in range(chunk):

                @pl.when(base + n > 0)
                def _():
                    pattern_copy(base + n).wait_recv()

        fields = seeds(base)
        for layer in reversed(range(slices)):
            ends = apply_both(table[1], table[0], fields)
            fields = []
            for n in range(chunk):
                back_real, back_imag = ends[n]
                col = off_ref[1, place[base + n]]
                if layer > 0:
                    psi_real = psis[layer - 1, base + n, 0].astype(jnp.float32)
                    psi_imag = psis[layer - 1, base + n, 1].astype(jnp.float32)
                    win_real = wins[layer - 1, base + n, 0]
                    win_imag = wins[layer - 1, base + n, 1]
                    fields.append(
                        (
                            (back_real * win_real + back_imag * win_imag).astype(jnp.bfloat16),
                            (back_imag * win_real - back_real * win_imag).astype(jnp.bfloat16),
                        )
                    )
                else:
                    psi_real = pr_ref[...].astype(jnp.float32)
                    psi_imag = pi_ref[...].astype(jnp.float32)
                terms = (
                    back_real * psi_real + back_imag * psi_imag,
                    back_imag * psi_real - back_real * psi_imag,
                )
                for plane in range(2):
                    rolled = pltpu.roll(terms[plane], lax.rem(col, LANES), axis=1)
                    pad[n, plane, 0, reach : reach + extent] = jnp.where(lane >= col, rolled, 0.0)
                    pad[n, plane, 1, reach : reach + extent] = jnp.where(lane < col, rolled, 0.0)
            for plane in range(2):
                for half in range(2):
                    total = acc[layer, plane, half]
                    for n in range(chunk):
                        start = reach - off_ref[0, place[base + n]]
                        total = total + pad[n, plane, half, pl.ds(start, height), :]
                    acc[layer, plane, half] = total

                    @pl.when((item == chunks - 1) & (cut != layer))
                    def _():
                        gsend[layer, plane, half] = acc[layer, plane, half].astype(jnp.bfloat16)
                        grad_to(layer, plane, half).start()

                    @pl.when((item == chunks - 1) & (cut == layer))
                    def _():
                        own_copy(layer, plane, half).start()

        return 0

    lax.fori_loop(0, chunks, ascend, 0)

    for step in order:
        request_copy(step).wait_send()
        pattern_copy(step).wait_send()
    for step in range(1, slices):
        slab_copy(step).wait_send()
    for plane in range(2):
        for half in range(2):
            own_copy(cut, plane, half).wait()
            for layer in range(slices):

                @pl.when(cut != layer)
                def _():
                    grad_to(layer, plane, half).wait_send()

            for step in range(1, slices):
                grad_copy(0, step, plane, half, lax.rem(cut + step, slices)).wait_recv()


def local(trans_real, trans_imag, probe_real, probe_imag, offsets, pattern_index, measured):
    extent = probe_real.shape[-1]
    positions = pattern_index.shape[0]
    tiles = lax.axis_size("tile")
    slices = lax.axis_size("cuts")
    height, width = trans_real.shape[1:]
    assert extent == LANES and width == 2 * LANES and trans_real.shape[0] == 1
    assert positions % slices == 0 and positions <= LANES
    assert tiles & (tiles - 1) == 0
    assert (positions + tiles - 1) // tiles <= slices
    count = positions // slices
    chunk = math.gcd(count, 4)
    exact = count == tiles

    others = slices - 1
    bf16, f32 = jnp.bfloat16, jnp.float32
    vmem = pl.BlockSpec(memory_space=pltpu.VMEM)
    smem = pl.BlockSpec(memory_space=pltpu.SMEM)
    hbm = pl.BlockSpec(memory_space=pl.ANY)
    dma = pltpu.SemaphoreType.DMA
    own, received = pl.pallas_call(
        functools.partial(kernel, tiles, slices, count, chunk, exact),
        out_shape=(
            jax.ShapeDtypeStruct((2, 1, height, width), f32),
            jax.ShapeDtypeStruct((others, 2, height, width), bf16),
        ),
        in_specs=[smem, vmem, vmem, vmem, hbm, hbm, hbm, hbm],
        out_specs=(hbm, hbm),
        scratch_shapes=[
            pltpu.VMEM(measured.shape, bf16),
            pltpu.VMEM((4, 2 * extent, 2 * extent), bf16),
            pltpu.SMEM((count,), jnp.int32),
            pltpu.SMEM((count,), jnp.int32),
            pltpu.VMEM((1, LANES), jnp.int32),
            pltpu.VMEM((slices, 2, 2, height, LANES), f32),
            pltpu.VMEM((2, 2, height, LANES), bf16),
            pltpu.VMEM((others, 2, 2, height, LANES), bf16),
            pltpu.VMEM((tiles, 1, LANES), jnp.int32),
            pltpu.VMEM((tiles, extent, extent), bf16),
            pltpu.VMEM((tiles, extent, extent), bf16),
            pltpu.VMEM((others, count, 2, extent, extent), f32),
            pltpu.VMEM((others, count, 2, extent, extent), bf16),
            pltpu.VMEM((count, 2, extent, extent), f32),
            pltpu.VMEM((chunk, 2, 2, 2 * height - extent, LANES), f32),
            pltpu.VMEM((slices, 2, 2, height, LANES), f32),
            pltpu.VMEM((slices, 2, 2, height, LANES), bf16),
            dma((6,)),
            dma((others,)),
            dma((others,)),
            dma((tiles,)),
            dma((tiles,)),
            dma((tiles,)),
            dma((tiles,)),
            dma((slices, 2, 2)),
            dma((others, 2, 2)),
            dma((2, 2)),
        ],
        compiler_params=pltpu.CompilerParams(
            collective_id=0, has_side_effects=True, vmem_limit_bytes=56 * 1024 * 1024
        ),
    )(
        offsets,
        pattern_index[None],
        probe_real,
        probe_imag,
        trans_real,
        trans_imag,
        measured,
        jnp.asarray(np.stack(tables(extent))),
    )
    return own + jnp.sum(received.astype(f32), axis=0)[:, None]


def solution(mesh):
    return jax.shard_map(
        local,
        mesh=mesh,
        in_specs=(
            P("cuts", "tile", None),
            P("cuts", "tile", None),
            P(),
            P(),
            P(None, "tile"),
            P("tile"),
            P("tile", None, None),
        ),
        out_specs=P(None, "cuts", "tile", None),
        check_vma=False,
    )
```
